32 devices in a mesh: region: 32 (over z, y, x, core).
Axes of the slice: x: 2, y: 2, z: 4, core: 2. Of those that a mesh axis runs over, the one named last changes fastest.
Arguments:
- node_feat: bfloat16 [16384, 512], P('region'), may hold values from -6 to 6
- edge_feat: bfloat16 [131072, 512], P('region'), may hold values from -6 to 6
- sender: int32 [131072], P('region'), may hold values from 0 to 1279, as said below
- receiver: int32 [131072], P('region'), may hold values from 0 to 512, as said below
- send_list: int32 [32, 8, 32], P('region'), may hold values from 16 to 511
- edge_w1: bfloat16 [1536, 512], replicated, may hold values from -0.15625 to 0.15625
- edge_b1: float32 [512], replicated, may hold values from -4 to 4
- edge_w2: bfloat16 [512, 512], replicated, may hold values from -0.25 to 0.25
- edge_b2: float32 [512], replicated, may hold values from -4 to 4
- edge_gain: float32 [512], replicated, may hold values from 0.5 to 1.5
- edge_shift: float32 [512], replicated, may hold values from -4 to 4
- node_w1: bfloat16 [1024, 512], replicated, may hold values from -0.1875 to 0.1875
- node_b1: float32 [512], replicated, may hold values from -4 to 4
- node_w2: bfloat16 [512, 512], replicated, may hold values from -0.25 to 0.25
- node_b2: float32 [512], replicated, may hold values from -4 to 4
- node_gain: float32 [512], replicated, may hold values from 0.5 to 1.5
- node_shift: float32 [512], replicated, may hold values from -4 to 4
Outputs:
- edge_out: bfloat16 [131072, 512], P('region')
- node_out: bfloat16 [16384, 512], P('region')
The draws below stay inside these ranges and needn't reach their ends.
Inputs may be any that keep to these rules, and one draw needn't show every extreme that they name: `sender`: a row of the region's table as built in the first step; every region has slots pointing at row 0 and at the last row. `receiver`: non-decreasing within each region's 4096 slots; the value 512 marks an empty slot, and empty slots stand after the used ones; some region uses all its slots. `send_list`: entry [s, j, k] is a local index on region s of a node that s sends to its j-th neighbour.
All inputs are finite; a program needn't handle non-finite values.
Results may differ from the reference program's by a relative error of at most 0.0043.
Values may be sent and summed in bfloat16 or wider, within the bound.
A program may use at most 128 MiB of HBM per device.

```python
import jax
import jax.numpy as jnp
from jax import lax

D = 512
NODE_DEV = 512
EDGE_DEV = 4096
COARSE_DEV = 16
NEIGH = 8
SLOT = 32
NODES = 16384
EDGES = 131072
TABLE = 1280
N_REGION = 32


def draw_sender(key, part):
    keys = jax.random.split(jax.random.fold_in(key, 11), 5)
    shape = (N_REGION, EDGE_DEV)
    kinds = jax.random.randint(keys[0], shape, 0, 10)
    local = jax.random.randint(keys[1], shape, 0, NODE_DEV)
    coarse = NODE_DEV + jax.random.randint(keys[2], shape, 0, COARSE_DEV * N_REGION)
    halo = NODE_DEV + COARSE_DEV * N_REGION + jax.random.randint(keys[3], shape, 0, NEIGH * SLOT)
    picked = jnp.where(kinds < 6, local, jnp.where(kinds < 8, coarse, halo))
    forced = jax.random.randint(keys[4], (N_REGION, 1), 0, EDGE_DEV)
    column = jnp.arange(EDGE_DEV, dtype=jnp.int32)[None, :]
    picked = jnp.where(column == forced, TABLE - 1, picked)
    picked = jnp.where(column == (forced + 1) % EDGE_DEV, 0, picked)
    return picked.reshape(-1).astype(jnp.int32)


def draw_receiver(key, part):
    keys = jax.random.split(jax.random.fold_in(key, 23), 3)
    levels = jax.random.randint(keys[0], (N_REGION,), 0, 4)
    divisor = jnp.array([1, 2, 4, 8], dtype=jnp.int32)[levels]
    live = EDGE_DEV // divisor
    full = jax.random.randint(keys[1], (), 0, N_REGION)
    rows = jnp.arange(N_REGION, dtype=jnp.int32)
    live = jnp.where(rows == full, EDGE_DEV, jnp.where(rows == (full + 1) % N_REGION, EDGE_DEV // 2, live))
    base = jnp.sort(jax.random.randint(keys[2], (N_REGION, EDGE_DEV), 0, NODE_DEV), axis=1)
    column = jnp.arange(EDGE_DEV, dtype=jnp.int32)[None, :]
    where_from = jnp.minimum(column * EDGE_DEV // live[:, None], EDGE_DEV - 1)
    chosen = jnp.take_along_axis(base, where_from, axis=1)
    chosen = jnp.where(column == 0, 0, chosen)
    chosen = jnp.where(column < live[:, None], chosen, NODE_DEV)
    return chosen.reshape(-1).astype(jnp.int32)


def set_ends(values, rng, smallest, top_value):
    place = [jax.random.randint(jax.random.fold_in(rng, axis), (), 0, length) for axis, length in enumerate(values.shape)]
    main_axis = values.shape.index(max(values.shape))
    neighbour = place[:main_axis] + [(place[main_axis] + 1) % values.shape[main_axis]] + place[main_axis + 1:]
    return values.at[tuple(place)].set(smallest).at[tuple(neighbour)].set(top_value)


def steps_of(stream_key, shape, cuts, low, top_value):
    def one(axis_at, blocks):
        draws = jax.random.uniform(jax.random.fold_in(jax.random.fold_in(stream_key, 6), axis_at), (blocks,), jnp.float32, low / len(cuts), top_value / len(cuts))
        return jnp.repeat(jnp.exp(draws), shape[axis_at] // blocks).reshape((-1,) + (1,) * (len(shape) - axis_at - 1))

    factor_of = one(*cuts[0])
    for cut in cuts[1:]:
        factor_of = factor_of * one(*cut)
    return factor_of


def noise(key, extent, width, most, cuts=(), kind=jnp.bfloat16):
    drawn = jax.random.normal(key, extent, jnp.float32) * width
    if len(cuts) > 0:
        drawn = steps_of(key, extent, cuts, -0.22, 0.18) * drawn
    return jnp.clip(drawn, min=-most, max=most).astype(kind)


def setup_inputs(seed: int = 0) -> dict:
    key_of = jax.random.split(jax.random.key(seed), 18)
    node_feat = noise(key_of[0], (NODES, D), 1.0, 6.0, ((0, 32),))
    edge_feat = noise(key_of[1], (EDGES, D), 1.0, 6.0, ((0, 32),))
    sender = draw_sender(jax.random.fold_in(key_of[17], 71), 0)
    receiver = draw_receiver(jax.random.fold_in(key_of[17], 71), 0)
    send_list = set_ends(jax.random.randint(key_of[4], (N_REGION, NEIGH, SLOT), COARSE_DEV, NODE_DEV), jax.random.fold_in(key_of[4], 1), COARSE_DEV, NODE_DEV - 1).astype(jnp.int32)
    edge_w1 = noise(key_of[5], (3 * D, D), (3 * D) ** -0.5, 0.15625)
    edge_b1 = noise(key_of[6], (D,), 1.0, 4.0, (), jnp.float32)
    edge_w2 = noise(key_of[7], (D, D), D ** -0.5, 0.25)
    edge_b2 = noise(key_of[8], (D,), 1.0, 4.0, (), jnp.float32)
    edge_gain = jnp.clip(1.0 + 0.1 * jax.random.normal(key_of[9], (D,), jnp.float32), 0.5, 1.5)
    edge_shift = noise(key_of[10], (D,), 1.0, 4.0, (), jnp.float32)
    node_w1 = noise(key_of[11], (2 * D, D), (2 * D) ** -0.5, 0.1875)
    node_b1 = noise(key_of[12], (D,), 1.0, 4.0, (), jnp.float32)
    node_w2 = noise(key_of[13], (D, D), D ** -0.5, 0.25)
    node_b2 = noise(key_of[14], (D,), 1.0, 4.0, (), jnp.float32)
    node_gain = jnp.clip(1.0 + 0.1 * jax.random.normal(key_of[15], (D,), jnp.float32), 0.5, 1.5)
    node_shift = noise(key_of[16], (D,), 1.0, 4.0, (), jnp.float32)
    return dict(node_feat=node_feat, edge_feat=edge_feat, sender=sender, receiver=receiver, send_list=send_list, edge_w1=edge_w1, edge_b1=edge_b1, edge_w2=edge_w2, edge_b2=edge_b2, edge_gain=edge_gain, edge_shift=edge_shift, node_w1=node_w1, node_b1=node_b1, node_w2=node_w2, node_b2=node_b2, node_gain=node_gain, node_shift=node_shift)


NEIGHBOUR_STEPS = (1, -1, 7, -7, 8, -8, 9, -9)

def network(inputs, w_first, b_first, w_second, b_second, gain, shift):
    pre = jnp.dot(inputs, w_first, preferred_element_type=jnp.float32) + b_first
    hidden = jax.nn.silu(pre).astype(jnp.bfloat16)
    out = jnp.dot(hidden, w_second, preferred_element_type=jnp.float32) + b_second
    mean = lax.optimization_barrier(jnp.mean(out, axis=-1, keepdims=True))
    var = lax.optimization_barrier(jnp.mean((out - mean) ** 2, axis=-1, keepdims=True))
    return (out - mean) * lax.rsqrt(var + 1e-05) * gain + shift

def reference(node_feat, edge_feat, sender, receiver, send_list, edge_w1, edge_b1, edge_w2, edge_b2, edge_gain, edge_shift, node_w1, node_b1, node_w2, node_b2, node_gain, node_shift):
    node_all = node_feat.reshape(N_REGION, NODE_DEV, D)
    edge_all = edge_feat.reshape(N_REGION, EDGE_DEV, D)
    send_all = sender.reshape(N_REGION, EDGE_DEV)
    recv_all = receiver.reshape(N_REGION, EDGE_DEV)
    coarse_all = node_all[:, :COARSE_DEV].reshape(-1, D)
    distances = jnp.array(NEIGHBOUR_STEPS, dtype=jnp.int32)
    positions = jnp.arange(NEIGH, dtype=jnp.int32)

    def region_update(region):
        local = node_all[region]
        sources = (region - distances) % N_REGION
        picks = send_list[sources, positions]
        halo = node_all[sources[:, None], picks].reshape(-1, D)
        table = jnp.concatenate([local, coarse_all, halo], axis=0)
        edges = edge_all[region]
        senders = send_all[region]
        receivers = recv_all[region]
        live = receivers < NODE_DEV
        recv_rows = jnp.take(local, jnp.minimum(receivers, NODE_DEV - 1), axis=0)
        inputs = jnp.concatenate([edges, jnp.take(table, senders, axis=0), recv_rows], axis=1)
        update = network(inputs, edge_w1, edge_b1, edge_w2, edge_b2, edge_gain, edge_shift)
        new_edges = jnp.where(live[:, None], edges.astype(jnp.float32) + update, 0.0).astype(jnp.bfloat16)
        aggregate = jax.ops.segment_sum(new_edges.astype(jnp.float32), receivers, num_segments=NODE_DEV + 1)[:NODE_DEV]
        node_in = jnp.concatenate([local, aggregate.astype(jnp.bfloat16)], axis=1)
        node_update = network(node_in, node_w1, node_b1, node_w2, node_b2, node_gain, node_shift)
        new_nodes = (local.astype(jnp.float32) + node_update).astype(jnp.bfloat16)
        return (new_edges, new_nodes)
    new_edges, new_nodes = lax.map(region_update, jnp.arange(N_REGION, dtype=jnp.int32))
    return (new_edges.reshape(EDGES, D), new_nodes.reshape(NODES, D))
```

```python
import functools

import jax
import jax.numpy as jnp
from jax import lax
from jax.experimental import pallas as pl
from jax.experimental.pallas import tpu as pltpu
from jax.sharding import PartitionSpec as P

COARSE_DEV = 16
NEIGHBOUR_STEPS = (1, -1, 7, -7, 8, -8, 9, -9)
MESH = pl.DeviceIdType.MESH
LANES = 128
F32 = jnp.float32
BF16 = jnp.bfloat16


def digits_of(n):
    bits = (n // 2).bit_length() - 1
    second = 1 << (bits // 2)
    return n // 2 // second, second, 2


def one_hot_rows(index_ref, first_group, groups, start, count):
    lane = lax.broadcasted_iota(jnp.int32, (LANES, LANES), 1)
    parts = []
    for g in range(groups):
        row = index_ref[pl.ds(first_group + g, 1), :]
        spread = jnp.broadcast_to(row, (LANES, LANES)).T - start
        parts.append(
            jnp.concatenate(
                [
                    jnp.where(spread == lane + c, 1.0, 0.0).astype(BF16)
                    for c in range(0, count, LANES)
                ],
                axis=1,
            )
        )
    return jnp.concatenate(parts, axis=0)


def one_hot_columns(index_ref, first_group, groups, count):
    parts = []
    for g in range(groups):
        row = index_ref[pl.ds(first_group + g, 1), :]
        ids = lax.broadcasted_iota(jnp.int32, (count, LANES), 0)
        parts.append(jnp.where(ids == row, 1.0, 0.0).astype(BF16))
    return jnp.concatenate(parts, axis=1)


def silu(x):
    half = 0.5 * x
    return half + half * jnp.tanh(half)


def layer_norm(y, gain, shift):
    inv = 1.0 / y.shape[1]
    y = y - jnp.sum(y, axis=1, keepdims=True) * inv
    var = jnp.sum(y * y, axis=1, keepdims=True) * inv
    return y * lax.rsqrt(var + 1e-5) * gain + shift


def exchange_kernel(
    n,
    block,
    node_hbm,
    edge_hbm,
    snd_ref,
    rcv_ref,
    sl_ref,
    w1_hbm,
    b1_ref,
    pre_hbm,
    coarse_out,
    halo_out,
    node_v,
    wsr_v,
    edge_v,
    pre_v,
    wcat,
    picked,
    load_sem,
    edge_sem,
    pre_sem,
    own_sem,
    send0,
    recv0,
    send1,
    recv1,
    send2,
    recv2,
    sendh,
    recvh,
):
    me = lax.axis_index("region")
    r0, r1, r2 = digits_of(n)
    d0, d1, d2 = me // (r1 * r2), (me // r2) % r1, me % r2
    nodes, width = node_v.shape
    blocks = edge_v.shape[0] // block
    groups = block // LANES
    neighbours, slots = sl_ref.shape

    def device(a, b, c):
        return ((a * r1 + b) * r2 + c,)

    def flip(d, k, r):
        out = jnp.int32(0)
        bit = 1
        while bit < r:
            have = (d // bit) % 2
            out = out + bit * (1 - have if k & bit else have)
            bit *= 2
        return out

    peers0 = [device(flip(d0, k, r0), d1, d2) for k in range(1, r0)]
    peers1 = [device(d0, flip(d1, k, r1), d2) for k in range(1, r1)]
    twin = device(d0, d1, 1 - d2)
    targets = [((me + step + n) % n,) for step in NEIGHBOUR_STEPS]

    load_node = pltpu.make_async_copy(node_hbm, node_v, load_sem.at[0])
    load_s = pltpu.make_async_copy(
        w1_hbm.at[pl.ds(width, width)], wsr_v.at[pl.ds(0, width)], load_sem.at[1]
    )
    load_r = pltpu.make_async_copy(
        w1_hbm.at[pl.ds(2 * width, width)], wsr_v.at[pl.ds(width, width)], load_sem.at[2]
    )
    load_e = pltpu.make_async_copy(
        w1_hbm.at[pl.ds(0, width)], wcat.at[pl.ds(0, width)], load_sem.at[3]
    )
    load_node.start()
    load_s.start()
    load_r.start()
    load_e.start()

    def edge_copy(i):
        rows = pl.ds(pl.multiple_of(i * block, block), block)
        return pltpu.make_async_copy(edge_hbm.at[rows], edge_v.at[rows], edge_sem.at[i])

    def pre_copy(i):
        rows = pl.ds(pl.multiple_of(i * block, block), block)
        return pltpu.make_async_copy(pre_v.at[rows], pre_hbm.at[rows], pre_sem.at[i])

    for i in range(blocks):
        edge_copy(i).start()

    barrier = pltpu.get_barrier_semaphore()
    greeted = peers0 + peers1 + [twin] + targets
    for target in greeted:
        pl.semaphore_signal(barrier, inc=1, device_id=target, device_id_type=MESH)

    load_node.wait()
    load_s.wait()
    sent_at = nodes + width
    wcat[pl.ds(sent_at, nodes), :] = jnp.dot(
        node_v[...], wsr_v[pl.ds(0, width), :], preferred_element_type=F32
    ).astype(BF16)

    mine = wcat.at[pl.ds(sent_at, COARSE_DEV)]
    own = pltpu.make_async_copy(mine, coarse_out.at[d0, d1, d2], own_sem)
    own.start()
    pl.semaphore_wait(barrier, len(greeted))
    stage0 = [
        pltpu.make_async_remote_copy(
            src_ref=mine,
            dst_ref=coarse_out.at[d0, d1, d2],
            send_sem=send0.at[k],
            recv_sem=recv0.at[k],
            device_id=peer,
            device_id_type=MESH,
        )
        for k, peer in enumerate(peers0)
    ]
    for copy in stage0:
        copy.start()

    ids = lax.broadcasted_iota(jnp.int32, (nodes, slots), 0)
    halo = []
    for j, target in enumerate(targets):
        wanted = jnp.where(ids == sl_ref[j : j + 1, :], 1.0, 0.0).astype(BF16)
        picked[j] = lax.dot_general(
            wanted,
            wcat[pl.ds(sent_at, nodes), :],
            (((0,), (0,)), ((), ())),
            preferred_element_type=F32,
        ).astype(BF16)
        copy = pltpu.make_async_remote_copy(
            src_ref=picked.at[j],
            dst_ref=halo_out.at[j],
            send_sem=sendh.at[j],
            recv_sem=recvh.at[j],
            device_id=target,
            device_id_type=MESH,
        )
        copy.start()
        halo.append(copy)

    load_r.wait()
    load_e.wait()
    wcat[pl.ds(width, nodes), :] = jnp.dot(
        node_v[...], wsr_v[pl.ds(width, width), :], preferred_element_type=F32
    ).astype(BF16)

    def one_block(i, carry):
        edge_copy(i).wait()
        rows = pl.ds(pl.multiple_of(i * block, block), block)
        left = jnp.concatenate(
            [
                edge_v[rows, :],
                one_hot_rows(rcv_ref, i * groups, groups, 0, nodes),
                one_hot_rows(snd_ref, i * groups, groups, 0, nodes),
            ],
            axis=1,
        )
        pre_v[rows, :] = jnp.dot(left, wcat[...], preferred_element_type=F32) + b1_ref[...]
        pre_copy(i).start()
        return carry

    cut1, cut2 = blocks // 4, 5 * blocks // 8
    lax.fori_loop(0, cut1, one_block, 0)

    own.wait()
    for copy in stage0:
        copy.wait_recv()

    def column_to(peer, digit, send_sem, recv_sem):
        column = coarse_out.at[:, digit, d2]
        return pltpu.make_async_remote_copy(
            src_ref=column,
            dst_ref=column,
            send_sem=send_sem,
            recv_sem=recv_sem,
            device_id=peer,
            device_id_type=MESH,
        )

    stage1 = [
        column_to(peer, d1, send1.at[k], recv1.at[k]) for k, peer in enumerate(peers1)
    ]
    stage2 = [
        column_to(twin, flip(d1, m, r1), send2.at[m], recv2.at[m]) for m in range(r1)
    ]
    for copy in stage1:
        copy.start()
    stage2[0].start()

    lax.fori_loop(cut1, cut2, one_block, 0)
    for k, copy in enumerate(stage1):
        copy.wait_recv()
        stage2[k + 1].start()
    lax.fori_loop(cut2, blocks, one_block, 0)

    for i in range(blocks):
        pre_copy(i).wait()
    for copy in halo:
        copy.wait()
    for copy in stage2:
        copy.wait()
    for copy in stage0 + stage1:
        copy.wait_send()


def update_kernel(
    block,
    pre_hbm,
    edge_hbm,
    coarse_hbm,
    halo_hbm,
    node_hbm,
    snd_ref,
    rcv_ref,
    w2_hbm,
    b2_ref,
    gain_ref,
    shift_ref,
    nw1_hbm,
    nb1_ref,
    nw2_hbm,
    nb2_ref,
    ngain_ref,
    nshift_ref,
    edge_out,
    node_out,
    pre_v,
    edge_v,
    out_v,
    table,
    node_v,
    w2_v,
    nw1_v,
    nw2_v,
    total,
    load_sem,
    pre_sem,
    edge_sem,
    out_sem,
):
    nodes, width = node_v.shape
    blocks = edge_v.shape[0] // block
    groups = block // LANES
    coarse_rows = coarse_hbm.shape[0]
    halo_rows = halo_hbm.shape[0]

    def rows_of(i):
        return pl.ds(pl.multiple_of(i * block, block), block)

    def pre_copy(i):
        rows = rows_of(i)
        return pltpu.make_async_copy(pre_hbm.at[rows], pre_v.at[rows], pre_sem.at[i])

    def edge_copy(i):
        rows = rows_of(i)
        return pltpu.make_async_copy(edge_hbm.at[rows], edge_v.at[rows], edge_sem.at[i])

    def out_copy(i):
        rows = rows_of(i)
        return pltpu.make_async_copy(out_v.at[rows], edge_out.at[rows], out_sem.at[i])

    loads = [
        pltpu.make_async_copy(source, place, load_sem.at[k])
        for k, (source, place) in enumerate(
            [
                (coarse_hbm, table.at[pl.ds(0, coarse_rows)]),
                (halo_hbm, table.at[pl.ds(coarse_rows, halo_rows)]),
                (w2_hbm, w2_v),
                (node_hbm, node_v),
                (nw1_hbm, nw1_v),
                (nw2_hbm, nw2_v),
            ]
        )
    ]
    for load in loads[:2]:
        load.start()
    pre_copy(0).start()
    loads[2].start()
    edge_copy(0).start()
    for i in range(1, blocks):
        pre_copy(i).start()
        edge_copy(i).start()
    for load in loads[3:]:
        load.start()
    total[...] = jnp.zeros_like(total)
    for load in loads[:3]:
        load.wait()

    def one_block(i, carry):
        pre_copy(i).wait()
        edge_copy(i).wait()
        rows = rows_of(i)
        wanted = one_hot_rows(snd_ref, i * groups, groups, nodes, coarse_rows + halo_rows)
        pre = pre_v[rows, :] + jnp.dot(wanted, table[...], preferred_element_type=F32)
        hidden = silu(pre).astype(BF16)
        y = jnp.dot(hidden, w2_v[...], preferred_element_type=F32) + b2_ref[...]
        new = edge_v[rows, :].astype(F32) + layer_norm(y, gain_ref[...], shift_ref[...])
        live = []
        for g in range(groups):
            row = rcv_ref[pl.ds(i * groups + g, 1), :]
            live.append(jnp.broadcast_to(row, (LANES, LANES)).T[:, :1])
        live = jnp.concatenate(live, axis=0) < nodes
        new = jnp.where(live, new, 0.0).astype(BF16)
        out_v[rows, :] = new
        out_copy(i).start()
        total[...] += jnp.dot(
            one_hot_columns(rcv_ref, i * groups, groups, nodes),
            new,
            preferred_element_type=F32,
        )
        return carry

    lax.fori_loop(0, blocks, one_block, 0)

    for load in loads[3:]:
        load.wait()
    node = node_v[...]
    both = jnp.concatenate([node, total[...].astype(BF16)], axis=1)
    pre = jnp.dot(both, nw1_v[...], preferred_element_type=F32) + nb1_ref[...]
    y = jnp.dot(silu(pre).astype(BF16), nw2_v[...], preferred_element_type=F32) + nb2_ref[...]
    node_out[...] = (
        node.astype(F32) + layer_norm(y, ngain_ref[...], nshift_ref[...])
    ).astype(BF16)
    for i in range(blocks):
        out_copy(i).wait()


def on_device(
    node_feat,
    edge_feat,
    sender,
    receiver,
    send_list,
    edge_w1,
    edge_b1,
    edge_w2,
    edge_b2,
    edge_gain,
    edge_shift,
    node_w1,
    node_b1,
    node_w2,
    node_b2,
    node_gain,
    node_shift,
):
    n = lax.axis_size("region")
    nodes, width = node_feat.shape
    edges = edge_feat.shape[0]
    neighbours, slots = send_list.shape[1:]
    block = min(512, edges)
    blocks = edges // block
    digits = digits_of(n)
    vmem = pl.BlockSpec(memory_space=pltpu.VMEM)
    hbm = pl.BlockSpec(memory_space=pl.ANY)
    dma = pltpu.SemaphoreType.DMA
    snd = sender.reshape(edges // LANES, LANES)
    rcv = receiver.reshape(edges // LANES, LANES)

    def row(vector):
        return vector.reshape(1, width)

    pre, coarse, halo = pl.pallas_call(
        functools.partial(exchange_kernel, n, block),
        out_shape=(
            jax.ShapeDtypeStruct((edges, width), F32),
            jax.ShapeDtypeStruct(digits + (COARSE_DEV, width), BF16),
            jax.ShapeDtypeStruct((neighbours, slots, width), BF16),
        ),
        in_specs=[hbm, hbm, vmem, vmem, vmem, hbm, vmem],
        out_specs=(hbm, hbm, hbm),
        scratch_shapes=[
            pltpu.VMEM((nodes, width), BF16),
            pltpu.VMEM((2 * width, width), BF16),
            pltpu.VMEM((edges, width), BF16),
            pltpu.VMEM((edges, width), F32),
            pltpu.VMEM((width + 2 * nodes, width), BF16),
            pltpu.VMEM((neighbours, slots, width), BF16),
            dma((4,)),
            dma((blocks,)),
            dma((blocks,)),
            dma,
            dma((digits[0] - 1,)),
            dma((digits[0] - 1,)),
            dma((digits[1] - 1,)),
            dma((digits[1] - 1,)),
            dma((digits[1],)),
            dma((digits[1],)),
            dma((neighbours,)),
            dma((neighbours,)),
        ],
        compiler_params=pltpu.CompilerParams(
            collective_id=0, has_side_effects=True, vmem_limit_bytes=48 * 2**20
        ),
        cost_estimate=pl.CostEstimate(
            flops=2 * edges * (width + 2 * nodes) * width,
            bytes_accessed=6 * edges * width,
            transcendentals=0,
        ),
        name="exchange",
    )(node_feat, edge_feat, snd, rcv, send_list[0], edge_w1, row(edge_b1))

    coarse_rows = n * COARSE_DEV
    halo_rows = neighbours * slots
    return pl.pallas_call(
        functools.partial(update_kernel, block),
        out_shape=(
            jax.ShapeDtypeStruct((edges, width), BF16),
            jax.ShapeDtypeStruct((nodes, width), BF16),
        ),
        in_specs=[hbm] * 5 + [vmem] * 2 + [hbm] + [vmem] * 3 + [hbm, vmem, hbm] + [vmem] * 3,
        out_specs=(hbm, vmem),
        scratch_shapes=[
            pltpu.VMEM((edges, width), F32),
            pltpu.VMEM((edges, width), BF16),
            pltpu.VMEM((edges, width), BF16),
            pltpu.VMEM((coarse_rows + halo_rows, width), BF16),
            pltpu.VMEM((nodes, width), BF16),
            pltpu.VMEM(edge_w2.shape, BF16),
            pltpu.VMEM(node_w1.shape, BF16),
            pltpu.VMEM(node_w2.shape, BF16),
            pltpu.VMEM((nodes, width), F32),
            dma((6,)),
            dma((blocks,)),
            dma((blocks,)),
            dma((blocks,)),
        ],
        compiler_params=pltpu.CompilerParams(vmem_limit_bytes=48 * 2**20),
        cost_estimate=pl.CostEstimate(
            flops=2 * edges * (2 * width + coarse_rows + halo_rows) * width,
            bytes_accessed=8 * edges * width,
            transcendentals=edges * width,
        ),
        name="update",
    )(
        pre,
        edge_feat,
        coarse.reshape(coarse_rows, width),
        halo.reshape(halo_rows, width),
        node_feat,
        snd,
        rcv,
        edge_w2,
        row(edge_b2),
        row(edge_gain),
        row(edge_shift),
        node_w1,
        row(node_b1),
        node_w2,
        row(node_b2),
        row(node_gain),
        row(node_shift),
    )


def solution(mesh):
    split2, split1, whole = P("region", None), P("region"), P()
    in_specs = (split2, split2, split1, split1, P("region", None, None)) + (whole,) * 12
    return jax.shard_map(
        on_device, mesh=mesh, in_specs=in_specs, out_specs=(split2, split2), check_vma=False
    )
```

```python
import functools

import jax
import jax.numpy as jnp
from jax import lax
from jax.experimental import pallas as pl
from jax.experimental.pallas import tpu as pltpu
from jax.sharding import PartitionSpec as P

COARSE_DEV = 16
NEIGHBOUR_STEPS = (1, -1, 7, -7, 8, -8, 9, -9)
MESH = pl.DeviceIdType.MESH
LANES = 128
VMEM_BYTES = 64 * 2**20
F32 = jnp.float32
BF16 = jnp.bfloat16


def digits_of(n):
    bits = (n // 2).bit_length() - 1
    second = 1 << (bits // 2)
    return n // 2 // second, second, 2


def one_hot_rows(index_ref, first_group, groups, start, count):
    lane = lax.broadcasted_iota(jnp.int32, (LANES, LANES), 1).astype(jnp.int16)
    one, zero = jnp.ones((), BF16), jnp.zeros((), BF16)
    parts = []
    for g in range(groups):
        row = index_ref[pl.ds(first_group + g, 1), :] - start
        spread = jnp.broadcast_to(row, (LANES, LANES)).T.astype(jnp.int16) - lane
        parts.append(
            jnp.concatenate(
                [jnp.where(spread == c, one, zero) for c in range(0, count, LANES)], axis=1
            )
        )
    return jnp.concatenate(parts, axis=0)


def one_hot_columns(index_ref, first_group, groups, start, count):
    lane = lax.broadcasted_iota(jnp.int32, (LANES, LANES), 0)
    one, zero = jnp.ones((), BF16), jnp.zeros((), BF16)
    parts = []
    for g in range(groups):
        row = index_ref[pl.ds(first_group + g, 1), :] - start
        spread = (row - lane).astype(jnp.int16)
        parts.append(
            jnp.concatenate(
                [jnp.where(spread == c, one, zero) for c in range(0, count, LANES)], axis=0
            )
        )
    return jnp.concatenate(parts, axis=1)


def silu_of_half(half):
    return half + half * jnp.tanh(half)


def layer_norm(y, gain, shift):
    inv = 1.0 / y.shape[1]
    y = y - jnp.sum(y, axis=1, keepdims=True) * inv
    var = jnp.sum(y * y, axis=1, keepdims=True) * inv
    return y * lax.rsqrt(var + 1e-5) * gain + shift


def exchange_kernel(
    n,
    block,
    node_hbm,
    edge_hbm,
    snd_hbm,
    rcv_hbm,
    sl_hbm,
    w1_hbm,
    b1_hbm,
    pre_hbm,
    coarse_out,
    halo_out,
    snd_ref,
    rcv_ref,
    sl_ref,
    b1_ref,
    node_v,
    wsr_v,
    edge_v,
    pre_v,
    wcat,
    picked,
    load_sem,
    edge_sem,
    pre_sem,
    own_sem,
    send0,
    recv0,
    send1,
    recv1,
    send2,
    recv2,
    sendh,
    recvh,
):
    me = lax.axis_index("region")
    r0, r1, r2 = digits_of(n)
    d0, d1, d2 = me // (r1 * r2), (me // r2) % r1, me % r2
    nodes, width = node_v.shape
    blocks = edge_v.shape[0] // block
    groups = block // LANES
    neighbours, slots = sl_ref.shape

    def device(a, b, c):
        return ((a * r1 + b) * r2 + c,)

    def flip(d, k, r):
        out = jnp.int32(0)
        bit = 1
        while bit < r:
            have = (d // bit) % 2
            out = out + bit * (1 - have if k & bit else have)
            bit *= 2
        return out

    peers0 = [device(flip(d0, k, r0), d1, d2) for k in range(1, r0)]
    peers1 = [device(d0, flip(d1, k, r1), d2) for k in range(1, r1)]
    twin = device(d0, d1, 1 - d2)
    targets = [((me + step + n) % n,) for step in NEIGHBOUR_STEPS]

    load_node = pltpu.make_async_copy(node_hbm, node_v, load_sem.at[0])
    load_s = pltpu.make_async_copy(
        w1_hbm.at[pl.ds(width, width)], wsr_v.at[pl.ds(0, width)], load_sem.at[1]
    )
    load_r = pltpu.make_async_copy(
        w1_hbm.at[pl.ds(2 * width, width)], wsr_v.at[pl.ds(width, width)], load_sem.at[2]
    )
    load_e = pltpu.make_async_copy(
        w1_hbm.at[pl.ds(0, width)], wcat.at[pl.ds(0, width)], load_sem.at[3]
    )
    small = [
        pltpu.make_async_copy(source, place, load_sem.at[4 + k])
        for k, (source, place) in enumerate(
            [(sl_hbm, sl_ref), (b1_hbm, b1_ref), (snd_hbm, snd_ref), (rcv_hbm, rcv_ref)]
        )
    ]
    load_node.start()
    load_s.start()
    small[0].start()
    load_r.start()
    load_e.start()
    for load in small[1:]:
        load.start()

    def edge_copy(i):
        rows = pl.ds(pl.multiple_of(i * block, block), block)
        return pltpu.make_async_copy(edge_hbm.at[rows], edge_v.at[rows], edge_sem.at[i])

    def pre_copy(i):
        rows = pl.ds(pl.multiple_of(i * block, block), block)
        return pltpu.make_async_copy(pre_v.at[rows], pre_hbm.at[rows], pre_sem.at[i])

    for i in range(blocks):
        edge_copy(i).start()

    barrier = pltpu.get_barrier_semaphore()
    greeted = peers0 + peers1 + [twin] + targets
    for target in greeted:
        pl.semaphore_signal(barrier, inc=1, device_id=target, device_id_type=MESH)

    load_node.wait()
    load_s.wait()
    sent_at = nodes + width
    wcat[pl.ds(sent_at, nodes), :] = (
        0.5 * jnp.dot(node_v[...], wsr_v[pl.ds(0, width), :], preferred_element_type=F32)
    ).astype(BF16)

    mine = wcat.at[pl.ds(sent_at, COARSE_DEV)]
    own = pltpu.make_async_copy(mine, coarse_out.at[d0, d1, d2], own_sem)
    own.start()
    pl.semaphore_wait(barrier, len(greeted))
    stage0 = [
        pltpu.make_async_remote_copy(
            src_ref=mine,
            dst_ref=coarse_out.at[d0, d1, d2],
            send_sem=send0.at[k],
            recv_sem=recv0.at[k],
            device_id=peer,
            device_id_type=MESH,
        )
        for k, peer in enumerate(peers0)
    ]
    for copy in stage0:
        copy.start()

    small[0].wait()
    ids = lax.broadcasted_iota(jnp.int32, (nodes, slots), 0)
    halo = []
    for j, target in enumerate(targets):
        wanted = jnp.where(ids == sl_ref[j : j + 1, :], 1.0, 0.0).astype(BF16)
        picked[j] = lax.dot_general(
            wanted,
            wcat[pl.ds(sent_at, nodes), :],
            (((0,), (0,)), ((), ())),
            preferred_element_type=F32,
        ).astype(BF16)
        copy = pltpu.make_async_remote_copy(
            src_ref=picked.at[j],
            dst_ref=halo_out.at[j],
            send_sem=sendh.at[j],
            recv_sem=recvh.at[j],
            device_id=target,
            device_id_type=MESH,
        )
        copy.start()
        halo.append(copy)

    load_r.wait()
    load_e.wait()
    for load in small[1:]:
        load.wait()
    wcat[pl.ds(0, width), :] = wcat[pl.ds(0, width), :] * jnp.asarray(0.5, BF16)
    wcat[pl.ds(width, nodes), :] = (
        0.5 * jnp.dot(node_v[...], wsr_v[pl.ds(width, width), :], preferred_element_type=F32)
    ).astype(BF16)
    bias = 0.5 * b1_ref[...]

    def one_block(i, carry):
        edge_copy(i).wait()
        rows = pl.ds(pl.multiple_of(i * block, block), block)
        left = jnp.concatenate(
            [
                edge_v[rows, :],
                one_hot_rows(rcv_ref, i * groups, groups, 0, nodes),
                one_hot_rows(snd_ref, i * groups, groups, 0, nodes),
            ],
            axis=1,
        )
        pre_v[rows, :] = jnp.dot(left, wcat[...], preferred_element_type=F32) + bias
        pre_copy(i).start()
        return carry

    cut1, cut2 = blocks // 4, 5 * blocks // 8
    lax.fori_loop(0, cut1, one_block, 0)

    own.wait()
    for copy in stage0:
        copy.wait_recv()

    def column_to(peer, digit, send_sem, recv_sem):
        column = coarse_out.at[:, digit, d2]
        return pltpu.make_async_remote_copy(
            src_ref=column,
            dst_ref=column,
            send_sem=send_sem,
            recv_sem=recv_sem,
            device_id=peer,
            device_id_type=MESH,
        )

    stage1 = [
        column_to(peer, d1, send1.at[k], recv1.at[k]) for k, peer in enumerate(peers1)
    ]
    stage2 = [
        column_to(twin, flip(d1, m, r1), send2.at[m], recv2.at[m]) for m in range(r1)
    ]
    for copy in stage1:
        copy.start()
    stage2[0].start()

    lax.fori_loop(cut1, cut2, one_block, 0)
    for k, copy in enumerate(stage1):
        copy.wait_recv()
        stage2[k + 1].start()
    lax.fori_loop(cut2, blocks, one_block, 0)

    for i in range(blocks):
        pre_copy(i).wait()
    for copy in halo:
        copy.wait()
    for copy in stage2:
        copy.wait()
    for copy in stage0 + stage1:
        copy.wait_send()


def update_kernel(
    block,
    pre_hbm,
    edge_hbm,
    coarse_hbm,
    halo_hbm,
    node_hbm,
    snd_hbm,
    rcv_hbm,
    w2_hbm,
    b2_hbm,
    gain_hbm,
    shift_hbm,
    nw1_hbm,
    nb1_hbm,
    nw2_hbm,
    nb2_hbm,
    ngain_hbm,
    nshift_hbm,
    edge_out,
    node_out,
    pre_v,
    edge_v,
    out_v,
    table,
    snd_ref,
    rcv_ref,
    w2_v,
    rows_v,
    node_v,
    nw1_v,
    nw2_v,
    total,
    hidden_a,
    hidden_b,
    new_node,
    load_sem,
    pre_sem,
    edge_sem,
    out_sem,
):
    nodes, width = node_v.shape
    blocks = edge_v.shape[0] // block
    groups = block // LANES
    coarse_rows = coarse_hbm.shape[0]
    halo_rows = halo_hbm.shape[0]
    window = nodes // 2

    def rows_of(i):
        return pl.ds(pl.multiple_of(i * block, block), block)

    def pre_copy(i):
        rows = rows_of(i)
        return pltpu.make_async_copy(pre_hbm.at[rows], pre_v.at[rows], pre_sem.at[i])

    def edge_copy(i):
        rows = rows_of(i)
        return pltpu.make_async_copy(edge_hbm.at[rows], edge_v.at[rows], edge_sem.at[i])

    def out_copy(i):
        rows = rows_of(i)
        return pltpu.make_async_copy(out_v.at[rows], edge_out.at[rows], out_sem.at[i])

    pairs = [
        (coarse_hbm, table.at[pl.ds(0, coarse_rows)]),
        (snd_hbm, snd_ref),
        (halo_hbm, table.at[pl.ds(coarse_rows, halo_rows)]),
        (rcv_hbm, rcv_ref),
        (w2_hbm, w2_v),
        (b2_hbm, rows_v.at[0]),
        (gain_hbm, rows_v.at[1]),
        (shift_hbm, rows_v.at[2]),
        (nb1_hbm, rows_v.at[3]),
        (nb2_hbm, rows_v.at[4]),
        (ngain_hbm, rows_v.at[5]),
        (nshift_hbm, rows_v.at[6]),
        (node_hbm, node_v),
        (nw1_hbm, nw1_v),
        (nw2_hbm, nw2_v),
    ]
    loads = [
        pltpu.make_async_copy(source, place, load_sem.at[k])
        for k, (source, place) in enumerate(pairs)
    ]
    early, late = loads[:8], loads[8:]
    for load in loads[:3]:
        load.start()
    pre_copy(0).start()
    for load in loads[3:8]:
        load.start()
    edge_copy(0).start()
    for i in range(1, blocks):
        pre_copy(i).start()
        edge_copy(i).start()
    for load in late:
        load.start()
    total[...] = jnp.zeros_like(total)
    for load in early:
        load.wait()

    def first_layer(i, hidden):
        wanted = one_hot_rows(snd_ref, i * groups, groups, nodes, coarse_rows + halo_rows)
        half = pre_v[rows_of(i), :] + jnp.dot(
            wanted, table[...], preferred_element_type=F32
        )
        hidden[...] = silu_of_half(half).astype(BF16)

    def second_layer(i, hidden):
        y = jnp.dot(hidden[...], w2_v[...], preferred_element_type=F32) + rows_v[0]
        new = edge_v[rows_of(i), :].astype(F32) + layer_norm(y, rows_v[1], rows_v[2])
        live = []
        for g in range(groups):
            row = rcv_ref[pl.ds(i * groups + g, 1), :]
            live.append(jnp.broadcast_to(row, (LANES, LANES)).T[:, :1])
        live = jnp.concatenate(live, axis=0) < nodes
        out_v[rows_of(i), :] = jnp.where(live, new, 0.0).astype(BF16)

    def arrive(i):
        pre_copy(i).wait()
        edge_copy(i).wait()

    arrive(0)
    first_layer(0, hidden_a)

    def two_blocks(p, carry):
        i = 2 * p
        arrive(i + 1)
        arrive(i + 2)
        first_layer(i + 1, hidden_b)
        second_layer(i, hidden_a)
        first_layer(i + 2, hidden_a)
        second_layer(i + 1, hidden_b)
        out_copy(i).start()
        out_copy(i + 1).start()
        return carry

    lax.fori_loop(0, blocks // 2 - 1, two_blocks, 0)
    arrive(blocks - 1)
    first_layer(blocks - 1, hidden_b)
    second_layer(blocks - 2, hidden_a)
    second_layer(blocks - 1, hidden_b)
    out_copy(blocks - 2).start()
    out_copy(blocks - 1).start()

    def sum_block(i, carry):
        lowest = jnp.min(rcv_ref[pl.ds(i * groups, 1), :])
        highest = jnp.max(rcv_ref[pl.ds(i * groups + groups - 1, 1), :])
        for start in range(0, nodes, window):

            @pl.when(jnp.logical_and(lowest < start + window, highest >= start))
            def _():
                total[pl.ds(start, window), :] += jnp.dot(
                    one_hot_columns(rcv_ref, i * groups, groups, start, window),
                    out_v[rows_of(i), :],
                    preferred_element_type=F32,
                )

        return carry

    lax.fori_loop(0, blocks, sum_block, 0)

    for load in late:
        load.wait()
    node = node_v[...]
    both = jnp.concatenate([node, total[...].astype(BF16)], axis=1)
    half = 0.5 * (jnp.dot(both, nw1_v[...], preferred_element_type=F32) + rows_v[3])
    y = (
        jnp.dot(silu_of_half(half).astype(BF16), nw2_v[...], preferred_element_type=F32)
        + rows_v[4]
    )
    new_node[...] = (node.astype(F32) + layer_norm(y, rows_v[5], rows_v[6])).astype(BF16)
    last = pltpu.make_async_copy(new_node, node_out, load_sem.at[len(loads)])
    last.start()
    for i in range(blocks):
        out_copy(i).wait()
    last.wait()


def on_device(
    node_feat,
    edge_feat,
    sender,
    receiver,
    send_list,
    edge_w1,
    edge_b1,
    edge_w2,
    edge_b2,
    edge_gain,
    edge_shift,
    node_w1,
    node_b1,
    node_w2,
    node_b2,
    node_gain,
    node_shift,
):
    n = lax.axis_size("region")
    nodes, width = node_feat.shape
    edges = edge_feat.shape[0]
    neighbours, slots = send_list.shape[1:]
    block = min(512, edges)
    blocks = edges // block
    digits = digits_of(n)
    hbm = pl.BlockSpec(memory_space=pl.ANY)
    dma = pltpu.SemaphoreType.DMA
    snd = sender.reshape(edges // LANES, LANES)
    rcv = receiver.reshape(edges // LANES, LANES)

    def row(vector):
        return vector.reshape(1, width)

    pre, coarse, halo = pl.pallas_call(
        functools.partial(exchange_kernel, n, block),
        out_shape=(
            jax.ShapeDtypeStruct((edges, width), F32),
            jax.ShapeDtypeStruct(digits + (COARSE_DEV, width), BF16),
            jax.ShapeDtypeStruct((neighbours, slots, width), BF16),
        ),
        in_specs=[hbm] * 7,
        out_specs=(hbm, hbm, hbm),
        scratch_shapes=[
            pltpu.VMEM(snd.shape, jnp.int32),
            pltpu.VMEM(rcv.shape, jnp.int32),
            pltpu.VMEM((neighbours, slots), jnp.int32),
            pltpu.VMEM((1, width), F32),
            pltpu.VMEM((nodes, width), BF16),
            pltpu.VMEM((2 * width, width), BF16),
            pltpu.VMEM((edges, width), BF16),
            pltpu.VMEM((edges, width), F32),
            pltpu.VMEM((width + 2 * nodes, width), BF16),
            pltpu.VMEM((neighbours, slots, width), BF16),
            dma((8,)),
            dma((blocks,)),
            dma((blocks,)),
            dma,
            dma((digits[0] - 1,)),
            dma((digits[0] - 1,)),
            dma((digits[1] - 1,)),
            dma((digits[1] - 1,)),
            dma((digits[1],)),
            dma((digits[1],)),
            dma((neighbours,)),
            dma((neighbours,)),
        ],
        compiler_params=pltpu.CompilerParams(
            collective_id=0, has_side_effects=True, vmem_limit_bytes=VMEM_BYTES
        ),
        cost_estimate=pl.CostEstimate(
            flops=2 * edges * (width + 2 * nodes) * width,
            bytes_accessed=6 * edges * width,
            transcendentals=0,
        ),
        name="exchange",
    )(node_feat, edge_feat, snd, rcv, send_list[0], edge_w1, row(edge_b1))

    coarse_rows = n * COARSE_DEV
    halo_rows = neighbours * slots
    return pl.pallas_call(
        functools.partial(update_kernel, block),
        out_shape=(
            jax.ShapeDtypeStruct((edges, width), BF16),
            jax.ShapeDtypeStruct((nodes, width), BF16),
        ),
        in_specs=[hbm] * 17,
        out_specs=(hbm, hbm),
        scratch_shapes=[
            pltpu.VMEM((edges, width), F32),
            pltpu.VMEM((edges, width), BF16),
            pltpu.VMEM((edges, width), BF16),
            pltpu.VMEM((coarse_rows + halo_rows, width), BF16),
            pltpu.VMEM(snd.shape, jnp.int32),
            pltpu.VMEM(rcv.shape, jnp.int32),
            pltpu.VMEM(edge_w2.shape, BF16),
            pltpu.VMEM((7, 1, width), F32),
            pltpu.VMEM((nodes, width), BF16),
            pltpu.VMEM(node_w1.shape, BF16),
            pltpu.VMEM(node_w2.shape, BF16),
            pltpu.VMEM((nodes, width), F32),
            pltpu.VMEM((block, width), BF16),
            pltpu.VMEM((block, width), BF16),
            pltpu.VMEM((nodes, width), BF16),
            dma((16,)),
            dma((blocks,)),
            dma((blocks,)),
            dma((blocks,)),
        ],
        compiler_params=pltpu.CompilerParams(vmem_limit_bytes=VMEM_BYTES),
        cost_estimate=pl.CostEstimate(
            flops=2 * edges * (2 * width + coarse_rows + halo_rows) * width,
            bytes_accessed=8 * edges * width,
            transcendentals=edges * width,
        ),
        name="update",
    )(
        pre,
        edge_feat,
        coarse.reshape(coarse_rows, width),
        halo.reshape(halo_rows, width),
        node_feat,
        snd,
        rcv,
        edge_w2,
        row(edge_b2),
        row(edge_gain),
        row(edge_shift),
        node_w1,
        row(node_b1),
        node_w2,
        row(node_b2),
        row(node_gain),
        row(node_shift),
    )


def solution(mesh):
    split2, split1, whole = P("region", None), P("region"), P()
    in_specs = (split2, split2, split1, split1, P("region", None, None)) + (whole,) * 12
    return jax.shard_map(
        on_device, mesh=mesh, in_specs=in_specs, out_specs=(split2, split2), check_vma=False
    )
```

```python
import functools

import jax
import jax.numpy as jnp
from jax import lax
from jax.experimental import pallas as pl
from jax.experimental.pallas import tpu as pltpu
from jax.sharding import PartitionSpec as P

COARSE_DEV = 16
NEIGHBOUR_STEPS = (1, -1, 7, -7, 8, -8, 9, -9)
MESH = pl.DeviceIdType.MESH
LANES = 128
VMEM_BYTES = 64 * 2**20
F32 = jnp.float32
BF16 = jnp.bfloat16


def digits_of(n):
    bits = (n // 2).bit_length() - 1
    second = 1 << (bits // 2)
    return n // 2 // second, second, 2


def one_hot_rows(index_ref, first_group, groups, start, count):
    lane = lax.broadcasted_iota(jnp.int32, (LANES, LANES), 1).astype(jnp.int16)
    one, zero = jnp.ones((), BF16), jnp.zeros((), BF16)
    parts = []
    for g in range(groups):
        row = index_ref[pl.ds(first_group + g, 1), :] - start
        spread = jnp.broadcast_to(row, (LANES, LANES)).T.astype(jnp.int16) - lane
        parts.append(
            jnp.concatenate(
                [jnp.where(spread == c, one, zero) for c in range(0, count, LANES)], axis=1
            )
        )
    return jnp.concatenate(parts, axis=0)


def one_hot_columns(index_ref, first_group, groups, start, count):
    lane = lax.broadcasted_iota(jnp.int32, (LANES, LANES), 0)
    one, zero = jnp.ones((), BF16), jnp.zeros((), BF16)
    parts = []
    for g in range(groups):
        row = index_ref[pl.ds(first_group + g, 1), :] - start
        spread = (row - lane).astype(jnp.int16)
        parts.append(
            jnp.concatenate(
                [jnp.where(spread == c, one, zero) for c in range(0, count, LANES)], axis=0
            )
        )
    return jnp.concatenate(parts, axis=1)


def silu_of_half(half):
    return half + half * jnp.tanh(half)


def layer_norm(y, gain, shift):
    inv = 1.0 / y.shape[1]
    y = y - jnp.sum(y, axis=1, keepdims=True) * inv
    var = jnp.sum(y * y, axis=1, keepdims=True) * inv
    return y * lax.rsqrt(var + 1e-5) * gain + shift


def exchange_kernel(
    n,
    block,
    node_hbm,
    edge_hbm,
    snd_hbm,
    rcv_hbm,
    sl_hbm,
    w1_hbm,
    b1_hbm,
    pre_hbm,
    coarse_out,
    halo_out,
    snd_ref,
    rcv_ref,
    sl_ref,
    b1_ref,
    node_v,
    wsr_v,
    edge_v,
    pre_v,
    wcat,
    picked,
    load_sem,
    edge_sem,
    pre_sem,
    own_sem,
    send0,
    recv0,
    send1,
    recv1,
    send2,
    recv2,
    sendh,
    recvh,
):
    me = lax.axis_index("region")
    r0, r1, r2 = digits_of(n)
    d0, d1, d2 = me // (r1 * r2), (me // r2) % r1, me % r2
    nodes, width = node_v.shape
    blocks = edge_v.shape[0] // block
    groups = block // LANES
    neighbours, slots = sl_ref.shape

    def device(a, b, c):
        return ((a * r1 + b) * r2 + c,)

    def flip(d, k, r):
        out = jnp.int32(0)
        bit = 1
        while bit < r:
            have = (d // bit) % 2
            out = out + bit * (1 - have if k & bit else have)
            bit *= 2
        return out

    peers0 = [device(flip(d0, k, r0), d1, d2) for k in range(1, r0)]
    peers1 = [device(d0, flip(d1, k, r1), d2) for k in range(1, r1)]
    twin = device(d0, d1, 1 - d2)
    targets = [((me + step + n) % n,) for step in NEIGHBOUR_STEPS]

    load_node = pltpu.make_async_copy(node_hbm, node_v, load_sem.at[0])
    load_s = pltpu.make_async_copy(
        w1_hbm.at[pl.ds(width, width)], wsr_v.at[pl.ds(0, width)], load_sem.at[1]
    )
    load_r = pltpu.make_async_copy(
        w1_hbm.at[pl.ds(2 * width, width)], wsr_v.at[pl.ds(width, width)], load_sem.at[2]
    )
    load_e = pltpu.make_async_copy(
        w1_hbm.at[pl.ds(0, width)], wcat.at[pl.ds(0, width)], load_sem.at[3]
    )
    small = [
        pltpu.make_async_copy(source, place, load_sem.at[4 + k])
        for k, (source, place) in enumerate(
            [(sl_hbm, sl_ref), (b1_hbm, b1_ref), (snd_hbm, snd_ref), (rcv_hbm, rcv_ref)]
        )
    ]
    load_node.start()
    load_s.start()
    small[0].start()
    load_r.start()
    load_e.start()
    for load in small[1:]:
        load.start()

    def edge_copy(i):
        rows = pl.ds(pl.multiple_of(i * block, block), block)
        return pltpu.make_async_copy(edge_hbm.at[rows], edge_v.at[rows], edge_sem.at[i])

    def pre_copy(i):
        rows = pl.ds(pl.multiple_of(i * block, block), block)
        return pltpu.make_async_copy(pre_v.at[rows], pre_hbm.at[rows], pre_sem.at[i])

    barrier = pltpu.get_barrier_semaphore()
    greeted = peers0 + peers1 + [twin] + targets
    for target in greeted:
        pl.semaphore_signal(barrier, inc=1, device_id=target, device_id_type=MESH)

    load_node.wait()
    load_s.wait()
    small[0].wait()
    for i in range(blocks):
        edge_copy(i).start()
    sent_at = nodes + width
    wcat[pl.ds(sent_at, nodes), :] = (
        0.5 * jnp.dot(node_v[...], wsr_v[pl.ds(0, width), :], preferred_element_type=F32)
    ).astype(BF16)

    ids = lax.broadcasted_iota(jnp.int32, (nodes, slots), 0)
    for j in range(neighbours):
        wanted = jnp.where(ids == sl_ref[j : j + 1, :], 1.0, 0.0).astype(BF16)
        picked[j] = lax.dot_general(
            wanted,
            wcat[pl.ds(sent_at, nodes), :],
            (((0,), (0,)), ((), ())),
            preferred_element_type=F32,
        ).astype(BF16)

    load_r.wait()
    load_e.wait()
    for load in small[1:]:
        load.wait()
    wcat[pl.ds(0, width), :] = wcat[pl.ds(0, width), :] * jnp.asarray(0.5, BF16)
    wcat[pl.ds(width, nodes), :] = (
        0.5 * jnp.dot(node_v[...], wsr_v[pl.ds(width, width), :], preferred_element_type=F32)
    ).astype(BF16)
    bias = 0.5 * b1_ref[...]

    def one_block(i, carry):
        edge_copy(i).wait()
        rows = pl.ds(pl.multiple_of(i * block, block), block)
        left = jnp.concatenate(
            [
                edge_v[rows, :],
                one_hot_rows(rcv_ref, i * groups, groups, 0, nodes),
                one_hot_rows(snd_ref, i * groups, groups, 0, nodes),
            ],
            axis=1,
        )
        pre_v[rows, :] = jnp.dot(left, wcat[...], preferred_element_type=F32) + bias
        pre_copy(i).start()
        return carry

    cut0, cut1, cut2 = blocks // 8, 3 * blocks // 8, 5 * blocks // 8
    lax.fori_loop(0, cut0, one_block, 0)

    mine = wcat.at[pl.ds(sent_at, COARSE_DEV)]
    own = pltpu.make_async_copy(mine, coarse_out.at[d0, d1, d2], own_sem)
    own.start()
    pl.semaphore_wait(barrier, len(greeted))
    stage0 = [
        pltpu.make_async_remote_copy(
            src_ref=mine,
            dst_ref=coarse_out.at[d0, d1, d2],
            send_sem=send0.at[k],
            recv_sem=recv0.at[k],
            device_id=peer,
            device_id_type=MESH,
        )
        for k, peer in enumerate(peers0)
    ]
    halo = [
        pltpu.make_async_remote_copy(
            src_ref=picked.at[j],
            dst_ref=halo_out.at[j],
            send_sem=sendh.at[j],
            recv_sem=recvh.at[j],
            device_id=target,
            device_id_type=MESH,
        )
        for j, target in enumerate(targets)
    ]
    for copy in stage0 + halo:
        copy.start()

    lax.fori_loop(cut0, cut1, one_block, 0)

    own.wait()
    for copy in stage0:
        copy.wait_recv()

    def column_to(peer, digit, send_sem, recv_sem):
        column = coarse_out.at[:, digit, d2]
        return pltpu.make_async_remote_copy(
            src_ref=column,
            dst_ref=column,
            send_sem=send_sem,
            recv_sem=recv_sem,
            device_id=peer,
            device_id_type=MESH,
        )

    stage1 = [
        column_to(peer, d1, send1.at[k], recv1.at[k]) for k, peer in enumerate(peers1)
    ]
    stage2 = [
        column_to(twin, flip(d1, m, r1), send2.at[m], recv2.at[m]) for m in range(r1)
    ]
    for copy in stage1:
        copy.start()
    stage2[0].start()

    lax.fori_loop(cut1, cut2, one_block, 0)
    for k, copy in enumerate(stage1):
        copy.wait_recv()
        stage2[k + 1].start()
    lax.fori_loop(cut2, blocks, one_block, 0)

    for i in range(blocks):
        pre_copy(i).wait()
    for copy in halo:
        copy.wait()
    for copy in stage2:
        copy.wait()
    for copy in stage0 + stage1:
        copy.wait_send()


def update_kernel(
    block,
    pre_hbm,
    edge_hbm,
    coarse_hbm,
    halo_hbm,
    node_hbm,
    snd_hbm,
    rcv_hbm,
    w2_hbm,
    b2_hbm,
    gain_hbm,
    shift_hbm,
    nw1_hbm,
    nb1_hbm,
    nw2_hbm,
    nb2_hbm,
    ngain_hbm,
    nshift_hbm,
    edge_out,
    node_out,
    pre_v,
    edge_v,
    out_v,
    table,
    snd_ref,
    rcv_ref,
    w2_v,
    rows_v,
    node_v,
    nw1_v,
    nw2_v,
    total,
    hidden_a,
    hidden_b,
    sent,
    second,
    new_node,
    load_sem,
    pre_sem,
    edge_sem,
    out_sem,
):
    nodes, width = node_v.shape
    blocks = edge_v.shape[0] // block
    groups = block // LANES
    coarse_rows = coarse_hbm.shape[0]
    halo_rows = halo_hbm.shape[0]
    window = nodes // 2
    piece = 32

    def rows_of(i):
        return pl.ds(pl.multiple_of(i * block, block), block)

    def pre_copy(i):
        rows = rows_of(i)
        return pltpu.make_async_copy(pre_hbm.at[rows], pre_v.at[rows], pre_sem.at[i])

    def edge_copy(i):
        rows = rows_of(i)
        return pltpu.make_async_copy(edge_hbm.at[rows], edge_v.at[rows], edge_sem.at[i])

    def out_copy(i):
        rows = rows_of(i)
        return pltpu.make_async_copy(out_v.at[rows], edge_out.at[rows], out_sem.at[i])

    pairs = [
        (rcv_hbm, rcv_ref),
        (coarse_hbm, table.at[pl.ds(0, coarse_rows)]),
        (snd_hbm, snd_ref),
        (halo_hbm, table.at[pl.ds(coarse_rows, halo_rows)]),
        (w2_hbm, w2_v),
        (b2_hbm, rows_v.at[0]),
        (gain_hbm, rows_v.at[1]),
        (shift_hbm, rows_v.at[2]),
        (nb1_hbm, rows_v.at[3]),
        (nb2_hbm, rows_v.at[4]),
        (ngain_hbm, rows_v.at[5]),
        (nshift_hbm, rows_v.at[6]),
        (node_hbm, node_v),
        (nw1_hbm, nw1_v),
        (nw2_hbm, nw2_v),
    ]
    loads = [
        pltpu.make_async_copy(source, place, load_sem.at[k])
        for k, (source, place) in enumerate(pairs)
    ]
    early, late = loads[:8], loads[8:]
    def fetch(i):
        pre_copy(i).start()
        edge_copy(i).start()

    rcv_load, early = early[0], early[1:]
    rcv_load.start()
    for load in early[:3]:
        load.start()
    fetch(0)
    for load in early[3:]:
        load.start()
    fetch(1)
    rcv_load.wait()
    live_count = jnp.sum(jnp.where(rcv_ref[...] < nodes, 1, 0))
    live_pairs = jnp.maximum((live_count + 2 * block - 1) // (2 * block), 1)
    live_blocks = 2 * live_pairs

    @pl.when(live_pairs > 1)
    def _():
        fetch(2)
        fetch(3)

    for load in late:
        load.start()
    total[...] = jnp.zeros_like(total)

    def empty_block(i, carry):
        out_v[rows_of(i), :] = jnp.zeros((block, width), BF16)
        out_copy(i).start()
        return carry

    lax.fori_loop(live_blocks, blocks, empty_block, 0)
    for load in early:
        load.wait()
    row_ids = lax.broadcasted_iota(jnp.int32, (piece, width), 0)

    def sender_product(i):
        wanted = one_hot_rows(snd_ref, i * groups, groups, nodes, coarse_rows + halo_rows)
        sent[...] = jnp.dot(wanted, table[...], preferred_element_type=F32)

    def second_product(hidden):
        second[...] = jnp.dot(hidden[...], w2_v[...], preferred_element_type=F32)

    def activate(i, hidden):
        for at in range(0, block, piece):
            rows = pl.ds(pl.multiple_of(i * block + at, piece), piece)
            half = pre_v[rows, :] + sent[pl.ds(at, piece), :]
            hidden[pl.ds(at, piece), :] = silu_of_half(half).astype(BF16)

    def normalise(i):
        for at in range(0, block, piece):
            first = pl.multiple_of(i * block + at, piece)
            rows = pl.ds(first, piece)
            y = second[pl.ds(at, piece), :] + rows_v[0]
            new = edge_v[rows, :].astype(F32) + layer_norm(y, rows_v[1], rows_v[2])
            out_v[rows, :] = jnp.where(row_ids < live_count - first, new, 0.0).astype(BF16)

    def arrive(i):
        pre_copy(i).wait()
        edge_copy(i).wait()

    def step(i, hidden_now, hidden_next):
        second_product(hidden_now)
        sender_product(i + 1)
        normalise(i)
        activate(i + 1, hidden_next)

    arrive(0)
    sender_product(0)
    activate(0, hidden_a)

    def two_blocks(p, carry):
        i = 2 * p
        arrive(i + 1)
        arrive(i + 2)

        @pl.when(i + 4 < live_blocks)
        def _():
            fetch(i + 4)
            fetch(i + 5)

        step(i, hidden_a, hidden_b)
        step(i + 1, hidden_b, hidden_a)
        out_copy(i).start()
        out_copy(i + 1).start()
        return carry

    lax.fori_loop(0, live_pairs - 1, two_blocks, 0)
    arrive(live_blocks - 1)
    step(live_blocks - 2, hidden_a, hidden_b)
    second_product(hidden_b)
    normalise(live_blocks - 1)
    out_copy(live_blocks - 2).start()
    out_copy(live_blocks - 1).start()

    def sum_block(i, carry):
        lowest = jnp.min(rcv_ref[pl.ds(i * groups, 1), :])
        highest = jnp.max(rcv_ref[pl.ds(i * groups + groups - 1, 1), :])
        for start in range(0, nodes, window):

            @pl.when(jnp.logical_and(lowest < start + window, highest >= start))
            def _():
                total[pl.ds(start, window), :] += jnp.dot(
                    one_hot_columns(rcv_ref, i * groups, groups, start, window),
                    out_v[rows_of(i), :],
                    preferred_element_type=F32,
                )

        return carry

    lax.fori_loop(0, live_blocks, sum_block, 0)

    for load in late:
        load.wait()
    both = jnp.concatenate([node_v[...], total[...].astype(BF16)], axis=1)
    sent[...] = jnp.dot(both, nw1_v[...], preferred_element_type=F32)
    for at in range(0, nodes, piece):
        rows = pl.ds(at, piece)
        half = 0.5 * (sent[rows, :] + rows_v[3])
        hidden_a[rows, :] = silu_of_half(half).astype(BF16)
    second[...] = jnp.dot(hidden_a[...], nw2_v[...], preferred_element_type=F32)
    for at in range(0, nodes, piece):
        rows = pl.ds(at, piece)
        change = layer_norm(second[rows, :] + rows_v[4], rows_v[5], rows_v[6])
        new_node[rows, :] = (node_v[rows, :].astype(F32) + change).astype(BF16)
    last = pltpu.make_async_copy(new_node, node_out, load_sem.at[len(loads)])
    last.start()
    for i in range(blocks):
        out_copy(i).wait()
    last.wait()


def on_device(
    node_feat,
    edge_feat,
    sender,
    receiver,
    send_list,
    edge_w1,
    edge_b1,
    edge_w2,
    edge_b2,
    edge_gain,
    edge_shift,
    node_w1,
    node_b1,
    node_w2,
    node_b2,
    node_gain,
    node_shift,
):
    n = lax.axis_size("region")
    nodes, width = node_feat.shape
    edges = edge_feat.shape[0]
    neighbours, slots = send_list.shape[1:]
    block = min(nodes, edges)
    blocks = edges // block
    digits = digits_of(n)
    hbm = pl.BlockSpec(memory_space=pl.ANY)
    dma = pltpu.SemaphoreType.DMA
    snd = sender.reshape(edges // LANES, LANES)
    rcv = receiver.reshape(edges // LANES, LANES)

    def row(vector):
        return vector.reshape(1, width)

    pre, coarse, halo = pl.pallas_call(
        functools.partial(exchange_kernel, n, block),
        out_shape=(
            jax.ShapeDtypeStruct((edges, width), F32),
            jax.ShapeDtypeStruct(digits + (COARSE_DEV, width), BF16),
            jax.ShapeDtypeStruct((neighbours, slots, width), BF16),
        ),
        in_specs=[hbm] * 7,
        out_specs=(hbm, hbm, hbm),
        scratch_shapes=[
            pltpu.VMEM(snd.shape, jnp.int32),
            pltpu.VMEM(rcv.shape, jnp.int32),
            pltpu.VMEM((neighbours, slots), jnp.int32),
            pltpu.VMEM((1, width), F32),
            pltpu.VMEM((nodes, width), BF16),
            pltpu.VMEM((2 * width, width), BF16),
            pltpu.VMEM((edges, width), BF16),
            pltpu.VMEM((edges, width), F32),
            pltpu.VMEM((width + 2 * nodes, width), BF16),
            pltpu.VMEM((neighbours, slots, width), BF16),
            dma((8,)),
            dma((blocks,)),
            dma((blocks,)),
            dma,
            dma((digits[0] - 1,)),
            dma((digits[0] - 1,)),
            dma((digits[1] - 1,)),
            dma((digits[1] - 1,)),
            dma((digits[1],)),
            dma((digits[1],)),
            dma((neighbours,)),
            dma((neighbours,)),
        ],
        compiler_params=pltpu.CompilerParams(
            collective_id=0, has_side_effects=True, vmem_limit_bytes=VMEM_BYTES
        ),
        cost_estimate=pl.CostEstimate(
            flops=2 * edges * (width + 2 * nodes) * width,
            bytes_accessed=6 * edges * width,
            transcendentals=0,
        ),
        name="exchange",
    )(node_feat, edge_feat, snd, rcv, send_list[0], edge_w1, row(edge_b1))

    coarse_rows = n * COARSE_DEV
    halo_rows = neighbours * slots
    return pl.pallas_call(
        functools.partial(update_kernel, block),
        out_shape=(
            jax.ShapeDtypeStruct((edges, width), BF16),
            jax.ShapeDtypeStruct((nodes, width), BF16),
        ),
        in_specs=[hbm] * 17,
        out_specs=(hbm, hbm),
        scratch_shapes=[
            pltpu.VMEM((edges, width), F32),
            pltpu.VMEM((edges, width), BF16),
            pltpu.VMEM((edges, width), BF16),
            pltpu.VMEM((coarse_rows + halo_rows, width), BF16),
            pltpu.VMEM(snd.shape, jnp.int32),
            pltpu.VMEM(rcv.shape, jnp.int32),
            pltpu.VMEM(edge_w2.shape, BF16),
            pltpu.VMEM((7, 1, width), F32),
            pltpu.VMEM((nodes, width), BF16),
            pltpu.VMEM(node_w1.shape, BF16),
            pltpu.VMEM(node_w2.shape, BF16),
            pltpu.VMEM((nodes, width), F32),
            pltpu.VMEM((block, width), BF16),
            pltpu.VMEM((block, width), BF16),
            pltpu.VMEM((block, width), F32),
            pltpu.VMEM((block, width), F32),
            pltpu.VMEM((nodes, width), BF16),
            dma((16,)),
            dma((blocks,)),
            dma((blocks,)),
            dma((blocks,)),
        ],
        compiler_params=pltpu.CompilerParams(vmem_limit_bytes=VMEM_BYTES),
        cost_estimate=pl.CostEstimate(
            flops=2 * edges * (2 * width + coarse_rows + halo_rows) * width,
            bytes_accessed=8 * edges * width,
            transcendentals=edges * width,
        ),
        name="update",
    )(
        pre,
        edge_feat,
        coarse.reshape(coarse_rows, width),
        halo.reshape(halo_rows, width),
        node_feat,
        snd,
        rcv,
        edge_w2,
        row(edge_b2),
        row(edge_gain),
        row(edge_shift),
        node_w1,
        row(node_b1),
        node_w2,
        row(node_b2),
        row(node_gain),
        row(node_shift),
    )


def solution(mesh):
    split2, split1, whole = P("region", None), P("region"), P()
    in_specs = (split2, split2, split1, split1, P("region", None, None)) + (whole,) * 12
    return jax.shard_map(
        on_device, mesh=mesh, in_specs=in_specs, out_specs=(split2, split2), check_vma=False
    )
```
